512 devices in a mesh: row: 16 (over y, z_hi), col: 32 (over z_lo, x, core).
Axes of the slice: x: 4, y: 8, z: 8 (z_hi: 2, z_lo: 4; z = z_hi * 4 + z_lo), core: 2. Of those that a mesh axis runs over, the one named last changes fastest.
Arguments:
- inputs: bfloat16 [512, 12288], P('col', 'row'), may hold values from -6 to 6
- weight: bfloat16 [12288, 24576], P('row', 'col'), may hold values from -0.0546875 to 0.0546875
- grad_out: bfloat16 [512, 24576], P('row', 'col'), may hold values from -6 to 6
Outputs:
- activated: bfloat16 [512, 24576], P('row', 'col')
- input_grad: bfloat16 [512, 12288], P('col', 'row')
- weight_grad: bfloat16 [12288, 24576], P('row', 'col')
The draws below stay inside these ranges and needn't reach their ends.
All inputs are finite; a program needn't handle non-finite values.
Results may differ from the reference program's by a relative error of at most 0.0049.
Values may be sent and summed in bfloat16 or wider, within the bound.
No kernel may reach another device: no remote copies, remote signals or barrier semaphores. Data moves between devices by JAX's collectives and lax.ppermute only.
A program may use at most 64 MiB of HBM per device.

```python
import jax
import jax.numpy as jnp
from jax import lax

D = 12288
FF = 24576
TOKENS = 512


def spiked(array, stream_key, source, target, parts, factor):
    def block_of(position):
        return (jnp.arange(array.shape[position]) // (array.shape[position] // parts)).reshape((-1,) + (1,) * (array.ndim - 1 - position))

    near = jax.random.permutation(stream_key, parts)[block_of(target)]
    second = (block_of(target) + parts // 2) % parts
    return jnp.where((block_of(source) == near) | (block_of(source) == second), factor * array, array)


def steps_of(own_key, dims, shards, low, largest):
    def one(position, parts):
        heights = jax.random.uniform(jax.random.fold_in(jax.random.fold_in(own_key, 6), position), (parts,), jnp.float32, low / len(shards), largest / len(shards))
        return jnp.repeat(jnp.exp(heights), dims[position] // parts).reshape((-1,) + (1,) * (len(dims) - position - 1))

    gain = one(*shards[0])
    for cut in shards[1:]:
        gain = gain * one(*cut)
    return gain


def centred(stream_key, shape, width, limit, cuts=(), dtype=jnp.bfloat16):
    factor_of = steps_of(stream_key, shape, cuts, -0.22, 0.18) if cuts else 1.0
    result = jax.random.normal(stream_key, shape, jnp.float32) * width * factor_of
    return jnp.minimum(jnp.maximum(result, -limit), limit).astype(dtype)


def bell_draw_with(key, shape, spread, bound, shards, heavy, held_as=jnp.bfloat16):
    drawn = spread * jax.random.normal(key, shape, jnp.float32)
    if shards:
        drawn = drawn * steps_of(key, shape, shards, -0.22, 0.18)
    return jnp.clip(spiked(drawn, jax.random.fold_in(key, 3), *heavy), -bound, bound).astype(held_as)


def setup_inputs(seed: int = 0) -> dict:
    key_list = jax.random.split(jax.random.key(seed), 4)
    return {
        "inputs": bell_draw_with(key_list[0], (TOKENS, D), 1.0, 6.0, ((0, 32), (1, 16)), (1, 0, 32, 2.75)),
        "weight": centred(key_list[1], (D, FF), D ** -0.5, 0.0546875, ((0, 16), (1, 32))),
        "grad_out": bell_draw_with(key_list[2], (TOKENS, FF), 1.0, 6.0, ((0, 16), (1, 32)), (1, 0, 32, 2.75)),
    }


coeff = 0.7978845608028654


def gelu_value(preact):
    inner = coeff * (preact + 0.044715 * preact * preact * preact)
    return 0.5 * preact * (1.0 + jnp.tanh(inner))


def gelu_derivative(preact):
    inner = coeff * (preact + 0.044715 * preact * preact * preact)
    tangent = jnp.tanh(inner)
    return 0.5 * (1.0 + tangent) + 0.5 * preact * (1.0 - tangent * tangent) * coeff * (1.0 + 3.0 * 0.044715 * preact * preact)


def reference(inputs, weight, grad_out):
    preact = jnp.dot(inputs, weight, preferred_element_type=jnp.float32)
    activated = gelu_value(preact).astype(jnp.bfloat16)
    grad_pre = (grad_out.astype(jnp.float32) * gelu_derivative(preact)).astype(jnp.bfloat16)
    input_grad = lax.dot_general(grad_pre, weight, (((1,), (1,)), ((), ())), preferred_element_type=jnp.float32).astype(jnp.bfloat16)
    weight_grad = lax.dot_general(inputs, grad_pre, (((0,), (0,)), ((), ())), preferred_element_type=jnp.float32).astype(jnp.bfloat16)
    return activated, input_grad, weight_grad
```

```python
import jax
import jax.numpy as jnp
from jax import lax
from jax.sharding import Mesh, PartitionSpec as P

coeff = 0.7978845608028654
ROW = ("y", "h")
COL = ("l", "x", "c")


def gelu_parts(preact):
    inner = coeff * (preact + 0.044715 * preact * preact * preact)
    tangent = jnp.tanh(inner)
    value = 0.5 * preact * (1.0 + tangent)
    slope = 0.5 * (1.0 + tangent) + 0.5 * preact * (1.0 - tangent * tangent) * coeff * (
        1.0 + 3.0 * 0.044715 * preact * preact
    )
    return value, slope


def gather_rows(block, axes, count):
    return lax.all_to_all(jnp.tile(block, (count, 1)), axes, 0, 0, tiled=True)


def scatter_sum(partial, axes, count):
    parts = lax.all_to_all(partial.astype(jnp.bfloat16), axes, 0, 0, tiled=True)
    parts = parts.reshape(count, parts.shape[0] // count, parts.shape[1])
    return jnp.sum(parts.astype(jnp.float32), axis=0)


def local(inputs, weight, grad_out):
    full_inputs = gather_rows(inputs, COL, 32)
    preact = scatter_sum(
        jnp.dot(full_inputs, weight, preferred_element_type=jnp.float32), ROW, 16
    )
    value, slope = gelu_parts(preact)
    activated = value.astype(jnp.bfloat16)
    grad_pre = (grad_out.astype(jnp.float32) * slope).astype(jnp.bfloat16)
    full_grads = gather_rows(grad_pre, ROW, 16)
    input_grad = scatter_sum(
        lax.dot_general(
            full_grads, weight, (((1,), (1,)), ((), ())), preferred_element_type=jnp.float32
        ),
        COL,
        32,
    ).astype(jnp.bfloat16)
    weight_grad = lax.dot_general(
        full_inputs, full_grads, (((0,), (0,)), ((), ())), preferred_element_type=jnp.float32
    ).astype(jnp.bfloat16)
    return (activated, input_grad, weight_grad)


def solution(mesh):
    fine = Mesh(mesh.devices.reshape(8, 2, 4, 4, 2), ("y", "h", "l", "x", "c"))
    return jax.shard_map(
        local,
        mesh=fine,
        in_specs=(P(COL, ROW), P(ROW, COL), P(ROW, COL)),
        out_specs=(P(ROW, COL), P(COL, ROW), P(ROW, COL)),
        check_vma=False,
    )
```

```python
import jax
import jax.numpy as jnp
from jax import lax
from jax.sharding import Mesh, PartitionSpec as P

coeff = 0.7978845608028654
ROW = ("y", "h")
COL = ("l", "x", "c")
CHIPS = ("l", "x")
SWAP = ((0, 1), (1, 0))


def gelu_parts(preact):
    inner = coeff * (preact + 0.044715 * preact * preact * preact)
    tangent = jnp.tanh(inner)
    value = 0.5 * preact * (1.0 + tangent)
    slope = 0.5 * (1.0 + tangent) + 0.5 * preact * (1.0 - tangent * tangent) * coeff * (
        1.0 + 3.0 * 0.044715 * preact * preact
    )
    return value, slope


def exchange(blocks, axes):
    return lax.all_to_all(blocks, axes, 0, 0, tiled=True)


def project(tokens, weight):
    return jnp.dot(tokens, weight, preferred_element_type=jnp.float32).astype(jnp.bfloat16)


def project_back(grads, weight):
    return lax.dot_general(
        grads, weight, (((1,), (1,)), ((), ())), preferred_element_type=jnp.float32
    )


def sum_parts(parts, count):
    parts = parts.reshape(count, parts.shape[0] // count, parts.shape[1])
    return jnp.sum(parts.astype(jnp.float32), axis=0)


def local(inputs, weight, grad_out):
    core = lax.axis_index("c")
    own = exchange(jnp.tile(inputs, (16, 1)), CHIPS)
    other = lax.ppermute(own, "c", SWAP)
    own, other = own.reshape(16, 1, 16, 768), other.reshape(16, 1, 16, 768)
    full_inputs = jnp.concatenate(
        [jnp.where(core == 0, own, other), jnp.where(core == 0, other, own)], axis=1
    ).reshape(512, 768)

    preact = sum_parts(exchange(project(full_inputs, weight), ROW), 16)
    value, slope = gelu_parts(preact)
    activated = value.astype(jnp.bfloat16)
    grad_pre = (grad_out.astype(jnp.float32) * slope).astype(jnp.bfloat16)
    full_grads = exchange(jnp.tile(grad_pre, (16, 1)), ROW)

    by_core = full_grads.reshape(16, 2, 16, 768)
    first, second = by_core[:, 0].reshape(256, 768), by_core[:, 1].reshape(256, 768)
    grads_own = jnp.where(core == 0, first, second)
    grads_other = jnp.where(core == 0, second, first)
    sent = lax.ppermute(project_back(grads_other, weight).astype(jnp.bfloat16), "c", SWAP)
    chip_sum = project_back(grads_own, weight) + sent.astype(jnp.float32)
    input_grad = sum_parts(exchange(chip_sum.astype(jnp.bfloat16), CHIPS), 16).astype(jnp.bfloat16)

    weight_grad = lax.dot_general(
        full_inputs, full_grads, (((0,), (0,)), ((), ())), preferred_element_type=jnp.float32
    ).astype(jnp.bfloat16)
    return (activated, input_grad, weight_grad)


def solution(mesh):
    fine = Mesh(mesh.devices.reshape(8, 2, 4, 4, 2), ("y", "h", "l", "x", "c"))
    return jax.shard_map(
        local,
        mesh=fine,
        in_specs=(P(COL, ROW), P(ROW, COL), P(ROW, COL)),
        out_specs=(P(ROW, COL), P(COL, ROW), P(ROW, COL)),
        check_vma=False,
    )
```

```python
import jax
import jax.numpy as jnp
from jax import lax
from jax.experimental import pallas as pl
from jax.experimental.pallas import tpu as pltpu
from jax.sharding import Mesh, PartitionSpec as P

coeff = 0.7978845608028654
ROW = ("y", "h")
COL = ("l", "x", "c")
CHIPS = ("l", "x")
SWAP = ((0, 1), (1, 0))
VMEM = pl.BlockSpec(memory_space=pltpu.VMEM)


def gelu_parts(preact):
    inner = coeff * (preact + 0.044715 * preact * preact * preact)
    tangent = jnp.tanh(inner)
    value = 0.5 * preact * (1.0 + tangent)
    slope = 0.5 * (1.0 + tangent) + 0.5 * preact * (1.0 - tangent * tangent) * coeff * (
        1.0 + 3.0 * 0.044715 * preact * preact
    )
    return value, slope


def project_kernel(tokens, low, high, out):
    for at, weight in ((0, low), (768, high)):
        out[:, at : at + 768] = jnp.dot(
            tokens[...], weight[...], preferred_element_type=jnp.float32
        ).astype(jnp.bfloat16)


def middle_kernel(parts, grad_out, value_out, grads_out):
    preact = parts[0].astype(jnp.float32)
    for k in range(1, 16):
        preact += parts[k].astype(jnp.float32)
    value, slope = gelu_parts(preact)
    value_out[...] = value.astype(jnp.bfloat16)
    grads = (grad_out[...].astype(jnp.float32) * slope).astype(jnp.bfloat16)
    for k in range(16):
        grads_out[k] = grads


def back_kernel(grads, low, high, out):
    dims = (((1,), (1,)), ((), ()))
    out[...] = (
        lax.dot_general(grads[:, :768], low[...], dims, preferred_element_type=jnp.float32)
        + lax.dot_general(grads[:, 768:], high[...], dims, preferred_element_type=jnp.float32)
    ).astype(jnp.bfloat16)


def outer_kernel(tokens, grads, other_tokens, other_grads, out):
    dims = (((0,), (0,)), ((), ()))
    out[...] = (
        lax.dot_general(tokens[...], grads[:, :768], dims, preferred_element_type=jnp.float32)
        + lax.dot_general(
            other_tokens[...], other_grads[...], dims, preferred_element_type=jnp.float32
        )
    ).astype(jnp.bfloat16)


def sum_kernel(parts, out):
    total = parts[0].astype(jnp.float32)
    for k in range(1, 16):
        total += parts[k].astype(jnp.float32)
    out[...] = total.astype(jnp.bfloat16)


def call(kernel, shapes, *operands, flops=0):
    shapes = [jax.ShapeDtypeStruct(shape, jnp.bfloat16) for shape in shapes]
    moved = sum(2 * a.size for a in operands) + sum(2 * s.size for s in shapes)
    outs = pl.pallas_call(
        kernel,
        out_shape=shapes,
        in_specs=[VMEM] * len(operands),
        out_specs=[VMEM] * len(shapes),
        compiler_params=pltpu.CompilerParams(vmem_limit_bytes=24 * 2**20),
        cost_estimate=pl.CostEstimate(flops=flops, bytes_accessed=moved, transcendentals=0),
    )(*operands)
    return outs if len(outs) > 1 else outs[0]


def exchange(blocks, axes):
    return lax.all_to_all(blocks, axes, 0, 0, tiled=True)


def swap(block):
    return lax.ppermute(block, "c", SWAP)


def after(value, *others):
    return lax.optimization_barrier((value, *others))[0]


def local(inputs, weight, grad_out):
    core = lax.axis_index("c")
    copies = jnp.tile(inputs[None], (16, 1, 1))
    tokens = exchange(copies, CHIPS).reshape(256, 768)
    chip_weight = swap(after(weight, copies))
    out_low, out_high = grad_out[:16], grad_out[16:]
    out_pair = jnp.concatenate(
        [
            jnp.where(core == 0, out_low, out_high),
            swap(after(jnp.where(core == 0, out_high, out_low), copies)),
        ],
        axis=1,
    )

    partial = call(
        project_kernel, [(256, 1536)], after(tokens, out_pair), weight, chip_weight, flops=2 * 256 * 768 * 1536
    )
    parts = exchange(partial.reshape(16, 16, 1536), ROW)
    value, grad_copies = call(middle_kernel, [(16, 1536), (16, 16, 1536)], parts, out_pair)
    grads = exchange(grad_copies, ROW).reshape(256, 1536)

    back = call(back_kernel, [(256, 768)], grads, weight, chip_weight, flops=2 * 256 * 768 * 1536)
    input_grad = call(sum_kernel, [(16, 768)], exchange(back.reshape(16, 16, 768), CHIPS))

    value, tokens = after(value, back), after(tokens, back)
    mine, theirs = value[:, :768], swap(value[:, 768:])
    activated = jnp.concatenate(
        [jnp.where(core == 0, mine, theirs), jnp.where(core == 0, theirs, mine)]
    )
    weight_grad = call(
        outer_kernel,
        [(768, 768)],
        tokens,
        grads,
        swap(tokens),
        swap(after(grads[:, 768:], back)),
        flops=4 * 256 * 768 * 768,
    )
    return (activated, input_grad, weight_grad)


def solution(mesh):
    fine = Mesh(mesh.devices.reshape(8, 2, 4, 4, 2), ("y", "h", "l", "x", "c"))
    return jax.shard_map(
        local,
        mesh=fine,
        in_specs=(P(COL, ROW), P(ROW, COL), P(ROW, COL)),
        out_specs=(P(ROW, COL), P(COL, ROW), P(ROW, COL)),
        check_vma=False,
    )
```

```python
import jax
import jax.numpy as jnp
from jax import lax
from jax.experimental import pallas as pl
from jax.experimental.pallas import tpu as pltpu
from jax.sharding import Mesh, PartitionSpec as P

coeff = 0.7978845608028654
ROW = ("y", "h")
COL = ("l", "x", "c")
CHIPS = ("l", "x")
SWAP = ((0, 1), (1, 0))
VMEM = pl.BlockSpec(memory_space=pltpu.VMEM)


def gelu_parts(preact):
    inner = coeff * (preact + 0.044715 * preact * preact * preact)
    tangent = jnp.tanh(inner)
    value = 0.5 * preact * (1.0 + tangent)
    slope = 0.5 * (1.0 + tangent) + 0.5 * preact * (1.0 - tangent * tangent) * coeff * (
        1.0 + 3.0 * 0.044715 * preact * preact
    )
    return value, slope


def project_kernel(tokens, own, *refs):
    *pieces, out = refs
    out[:, :768] = jnp.dot(tokens[...], own[...], preferred_element_type=jnp.float32).astype(
        jnp.bfloat16
    )
    total, row = 0.0, 0
    for piece in pieces:
        rows = piece.shape[0] - 16
        total += jnp.dot(
            tokens[:, row : row + rows], piece[:rows], preferred_element_type=jnp.float32
        )
        row += rows
    out[:, 768:] = total.astype(jnp.bfloat16)


def add_kernel(parts, grad_out, first, second, wide, narrow):
    total = parts[0].astype(jnp.float32)
    for k in range(1, 8):
        total += parts[k].astype(jnp.float32)
    wide[...] = total
    narrow[:32] = total.astype(jnp.bfloat16)
    core = lax.axis_index("c")
    narrow[32:, :768] = jnp.where(core == 0, grad_out[:16], grad_out[16:])
    narrow[32:, 768:] = jnp.where(core == 0, first[-16:], second[-16:])


def middle_kernel(near, far, sent, mine, theirs, grads_out):
    half = lax.axis_index("h")
    preact = near[...] + far[:32].astype(jnp.float32)
    value, slope = gelu_parts(preact)
    value = value.astype(jnp.bfloat16)
    kept = jnp.where(half == 0, value[:16], value[16:])
    mine[...] = kept[:, :768]
    theirs[...] = kept[:, 768:]
    own, other = sent[32:].astype(jnp.float32), far[32:].astype(jnp.float32)
    low = (jnp.where(half == 0, own, other) * slope[:16]).astype(jnp.bfloat16)
    high = (jnp.where(half == 0, other, own) * slope[16:]).astype(jnp.bfloat16)
    for k in range(8):
        grads_out[k, :16] = low
        grads_out[k, 16:] = high


def pack_kernel(grads, theirs, packed):
    packed[:256] = grads[:, 768:]
    packed[256:] = theirs[...]


def back_kernel(grads, own, *refs):
    *pieces, out = refs
    dims = (((1,), (1,)), ((), ()))
    row = 0
    for piece in pieces:
        rows = piece.shape[0] - 16
        out[:, row : row + rows] = (
            lax.dot_general(
                grads[:, :768], own[row : row + rows], dims, preferred_element_type=jnp.float32
            )
            + lax.dot_general(grads[:, 768:], piece[:rows], dims, preferred_element_type=jnp.float32)
        ).astype(jnp.bfloat16)
        row += rows


def outer_kernel(tokens, grads, mine, other_tokens, other, weight_grad, activated):
    dims = (((0,), (0,)), ((), ()))
    weight_grad[...] = (
        lax.dot_general(tokens[...], grads[:, :768], dims, preferred_element_type=jnp.float32)
        + lax.dot_general(other_tokens[...], other[:256], dims, preferred_element_type=jnp.float32)
    ).astype(jnp.bfloat16)
    core = lax.axis_index("c")
    activated[pl.ds(pl.multiple_of(core * 16, 16), 16), :] = mine[...]
    activated[pl.ds(pl.multiple_of(16 - core * 16, 16), 16), :] = other[256:]


def sum_kernel(parts, out):
    total = parts[0].astype(jnp.float32)
    for k in range(1, 16):
        total += parts[k].astype(jnp.float32)
    out[...] = total.astype(jnp.bfloat16)


def call(kernel, shapes, *operands, flops=0):
    shapes = [jax.ShapeDtypeStruct(s, jnp.bfloat16) if isinstance(s, tuple) else s for s in shapes]
    moved = sum(a.size * a.dtype.itemsize for a in (*operands, *shapes))
    outs = pl.pallas_call(
        kernel,
        out_shape=shapes,
        in_specs=[VMEM] * len(operands),
        out_specs=[VMEM] * len(shapes),
        compiler_params=pltpu.CompilerParams(vmem_limit_bytes=12 * 2**20),
        cost_estimate=pl.CostEstimate(flops=flops, bytes_accessed=moved, transcendentals=0),
    )(*operands)
    return outs if len(outs) > 1 else outs[0]


def exchange(blocks, axes):
    return lax.all_to_all(blocks, axes, 0, 0, tiled=True)


def swap(block, axis="c"):
    return lax.ppermute(block, axis, SWAP)


def after(value, *others):
    return lax.optimization_barrier((value, *others))[0]


def local(inputs, weight, grad_out):
    copies = jnp.tile(inputs[None], (16, 1, 1))
    tokens = exchange(copies, CHIPS).reshape(256, 768)
    given, sent_weight = after(grad_out, copies), after(weight, copies)
    pieces = [
        swap(jnp.concatenate([sent_weight[384 * k : 384 * k + 384], given[16 * k : 16 * k + 16]]))
        for k in (0, 1)
    ]

    partial = call(
        project_kernel, [(256, 1536)], tokens, weight, *pieces, flops=2 * 256 * 768 * 1536
    )
    parts = exchange(partial.reshape(8, 32, 1536), ("y",))
    near, sent = call(
        add_kernel,
        [jax.ShapeDtypeStruct((32, 1536), jnp.float32), (48, 1536)],
        parts, grad_out, *pieces,
    )
    mine, theirs, grad_copies = call(
        middle_kernel,
        [(16, 768), (16, 768), (8, 32, 1536)],
        near, swap(sent, "h"), sent,
    )
    grads = exchange(grad_copies, ("y",)).reshape(256, 1536)

    back = call(
        back_kernel, [(256, 768)], grads, weight, *pieces, flops=2 * 256 * 768 * 1536
    )
    input_grad = call(sum_kernel, [(16, 768)], exchange(back.reshape(16, 16, 768), CHIPS))

    packed = call(pack_kernel, [(272, 768)], after(grads, back), theirs)
    weight_grad, activated = call(
        outer_kernel,
        [(768, 768), (32, 768)],
        tokens, grads, mine, swap(after(tokens, back)), swap(packed),
        flops=4 * 256 * 768 * 768,
    )
    return (activated, input_grad, weight_grad)


def solution(mesh):
    fine = Mesh(mesh.devices.reshape(8, 2, 4, 4, 2), ("y", "h", "l", "x", "c"))
    return jax.shard_map(
        local,
        mesh=fine,
        in_specs=(P(COL, ROW), P(ROW, COL), P(ROW, COL)),
        out_specs=(P(ROW, COL), P(COL, ROW), P(ROW, COL)),
        check_vma=False,
    )
```

```python
import jax
import jax.numpy as jnp
from jax import lax
from jax.experimental import pallas as pl
from jax.experimental.pallas import tpu as pltpu
from jax.sharding import Mesh, PartitionSpec as P

coeff = 0.7978845608028654
ROW = ("y", "h")
COL = ("l", "x", "c")
CHIPS = ("l", "x")
SWAP = ((0, 1), (1, 0))
VMEM = pl.BlockSpec(memory_space=pltpu.VMEM)


def gelu_parts(preact):
    inner = coeff * (preact + 0.044715 * preact * preact * preact)
    tangent = jnp.tanh(inner)
    value = 0.5 * preact * (1.0 + tangent)
    slope = 0.5 * (1.0 + tangent) + 0.5 * preact * (1.0 - tangent * tangent) * coeff * (
        1.0 + 3.0 * 0.044715 * preact * preact
    )
    return value, slope


def project_kernel(tokens, own, *refs):
    *pieces, out = refs
    out[:, :768] = jnp.dot(tokens[...], own[...], preferred_element_type=jnp.float32).astype(
        jnp.bfloat16
    )
    total, row = 0.0, 0
    for piece in pieces:
        rows = piece.shape[0] - 16
        total += jnp.dot(
            tokens[:, row : row + rows], piece[:rows], preferred_element_type=jnp.float32
        )
        row += rows
    out[:, 768:] = total.astype(jnp.bfloat16)


def add_kernel(parts, grad_out, first, second, wide, narrow):
    total = parts[0].astype(jnp.float32)
    for k in range(1, 8):
        total += parts[k].astype(jnp.float32)
    wide[...] = total
    narrow[:32] = total.astype(jnp.bfloat16)
    core = lax.axis_index("c")
    narrow[32:, :768] = jnp.where(core == 0, grad_out[:16], grad_out[16:])
    narrow[32:, 768:] = jnp.where(core == 0, first[-16:], second[-16:])


def middle_kernel(near, far, sent, mine, theirs, grads_out):
    half = lax.axis_index("h")
    preact = near[...] + far[:32].astype(jnp.float32)
    value, slope = gelu_parts(preact)
    value = value.astype(jnp.bfloat16)
    kept = jnp.where(half == 0, value[:16], value[16:])
    mine[...] = kept[:, :768]
    theirs[...] = kept[:, 768:]
    own, other = sent[32:].astype(jnp.float32), far[32:].astype(jnp.float32)
    low = (jnp.where(half == 0, own, other) * slope[:16]).astype(jnp.bfloat16)
    high = (jnp.where(half == 0, other, own) * slope[16:]).astype(jnp.bfloat16)
    for k in range(8):
        grads_out[k, :16] = low
        grads_out[k, 16:] = high


def pack_kernel(grads, theirs, packed):
    packed[:256] = grads[:, 768:]
    packed[256:] = theirs[...]


def back_kernel(grads, own, *refs):
    *pieces, out = refs
    dims = (((1,), (1,)), ((), ()))
    row = 0
    for piece in pieces:
        rows = piece.shape[0] - 16
        out[:, row : row + rows] = (
            lax.dot_general(
                grads[:, :768], own[row : row + rows], dims, preferred_element_type=jnp.float32
            )
            + lax.dot_general(grads[:, 768:], piece[:rows], dims, preferred_element_type=jnp.float32)
        ).astype(jnp.bfloat16)
        row += rows


def outer_kernel(tokens, grads, mine, other_tokens, other, weight_grad, activated):
    dims = (((0,), (0,)), ((), ()))
    weight_grad[...] = (
        lax.dot_general(tokens[...], grads[:, :768], dims, preferred_element_type=jnp.float32)
        + lax.dot_general(other_tokens[...], other[:256], dims, preferred_element_type=jnp.float32)
    ).astype(jnp.bfloat16)
    core = lax.axis_index("c")
    activated[pl.ds(pl.multiple_of(core * 16, 16), 16), :] = mine[...]
    activated[pl.ds(pl.multiple_of(16 - core * 16, 16), 16), :] = other[256:]


def sum_kernel(parts, out):
    total = parts[0].astype(jnp.float32)
    for k in range(1, 16):
        total += parts[k].astype(jnp.float32)
    out[...] = total.astype(jnp.bfloat16)


def call(kernel, shapes, *operands, flops=0):
    shapes = [jax.ShapeDtypeStruct(s, jnp.bfloat16) if isinstance(s, tuple) else s for s in shapes]
    moved = sum(a.size * a.dtype.itemsize for a in (*operands, *shapes))
    outs = pl.pallas_call(
        kernel,
        out_shape=shapes,
        in_specs=[VMEM] * len(operands),
        out_specs=[VMEM] * len(shapes),
        compiler_params=pltpu.CompilerParams(vmem_limit_bytes=12 * 2**20),
    )(*operands)
    return outs if len(outs) > 1 else outs[0]


def exchange(blocks, axes):
    return lax.all_to_all(blocks, axes, 0, 0, tiled=True)


def swap(block, axis="c"):
    return lax.ppermute(block, axis, SWAP)


def after(value, *others):
    return lax.optimization_barrier((value, *others))[0]


def local(inputs, weight, grad_out):
    copies = jnp.tile(inputs[None], (16, 1, 1))
    tokens = exchange(copies, CHIPS).reshape(256, 768)
    given, sent_weight = after(grad_out, copies), after(weight, copies)
    pieces = [
        swap(jnp.concatenate([sent_weight[384 * k : 384 * k + 384], given[16 * k : 16 * k + 16]]))
        for k in (0, 1)
    ]

    partial = call(
        project_kernel, [(256, 1536)], tokens, weight, *pieces, flops=2 * 256 * 768 * 1536
    )
    parts = exchange(partial.reshape(8, 32, 1536), ("y",))
    near, sent = call(
        add_kernel,
        [jax.ShapeDtypeStruct((32, 1536), jnp.float32), (48, 1536)],
        parts, grad_out, *pieces,
    )
    mine, theirs, grad_copies = call(
        middle_kernel,
        [(16, 768), (16, 768), (8, 32, 1536)],
        near, swap(sent, "h"), sent,
    )
    grads = exchange(grad_copies, ("y",)).reshape(256, 1536)

    back = call(
        back_kernel, [(256, 768)], grads, weight, *pieces, flops=2 * 256 * 768 * 1536
    )
    input_grad = call(sum_kernel, [(16, 768)], exchange(back.reshape(16, 16, 768), CHIPS))

    packed = call(pack_kernel, [(272, 768)], after(grads, back), theirs)
    weight_grad, activated = call(
        outer_kernel,
        [(768, 768), (32, 768)],
        tokens, grads, mine, swap(after(tokens, back)), swap(packed),
        flops=4 * 256 * 768 * 768,
    )
    return (activated, input_grad, weight_grad)


def solution(mesh):
    fine = Mesh(mesh.devices.reshape(8, 2, 4, 4, 2), ("y", "h", "l", "x", "c"))
    return jax.shard_map(
        local,
        mesh=fine,
        in_specs=(P(COL, ROW), P(ROW, COL), P(ROW, COL)),
        out_specs=(P(ROW, COL), P(COL, ROW), P(ROW, COL)),
        check_vma=False,
    )
```

```python
import jax
import jax.numpy as jnp
from jax import lax
from jax.experimental import pallas as pl
from jax.experimental.pallas import tpu as pltpu
from jax.sharding import Mesh, PartitionSpec as P

coeff = 0.7978845608028654
Y = ("a", "b")
ROW = ("a", "b", "h")
COL = ("l", "x", "c")
CHIPS = ("l", "x")
SWAP = ((0, 1), (1, 0))
VMEM = pl.BlockSpec(memory_space=pltpu.VMEM)


def gelu_parts(preact):
    inner = coeff * (preact + 0.044715 * preact * preact * preact)
    tangent = jnp.tanh(inner)
    value = 0.5 * preact * (1.0 + tangent)
    slope = 0.5 * (1.0 + tangent) + 0.5 * preact * (1.0 - tangent * tangent) * coeff * (
        1.0 + 3.0 * 0.044715 * preact * preact
    )
    return value, slope


def gather_rows(tokens, rows, parity):
    for k in range(4):
        rows[32 * k : 32 * k + 32] = tokens[2 * k + parity]


def high_product(rows, first, second):
    return jnp.dot(rows[:, :384], first[:384], preferred_element_type=jnp.float32) + jnp.dot(
        rows[:, 384:], second[:384], preferred_element_type=jnp.float32
    )


def low_away_kernel(tokens, own, out, rows):
    gather_rows(tokens, rows, 1 - lax.axis_index("b"))
    out[...] = jnp.dot(rows[...], own[...], preferred_element_type=jnp.float32).astype(jnp.bfloat16)


def high_away_kernel(tokens, first, second, out, rows):
    gather_rows(tokens, rows, 1 - lax.axis_index("b"))
    out[...] = high_product(rows, first, second).astype(jnp.bfloat16)


def kept_kernel(tokens, own, first, second, kept, rows):
    gather_rows(tokens, rows, lax.axis_index("b"))
    kept[:, :768] = jnp.dot(rows[...], own[...], preferred_element_type=jnp.float32)
    kept[:, 768:] = high_product(rows, first, second)


def pair_kernel(kept, low, high, out):
    out[:, :768] = (kept[:, :768] + low[...].astype(jnp.float32)).astype(jnp.bfloat16)
    out[:, 768:] = (kept[:, 768:] + high[...].astype(jnp.float32)).astype(jnp.bfloat16)


def rows_kernel(grad_out, first, second, out):
    core = lax.axis_index("c")
    out[:, :768] = jnp.where(core == 0, grad_out[:16], grad_out[16:])
    out[:, 768:] = jnp.where(core == 0, first[-16:], second[-16:])


def add_kernel(parts, wide, narrow):
    total = parts[0].astype(jnp.float32)
    for k in range(1, 4):
        total += parts[k].astype(jnp.float32)
    wide[...] = total
    narrow[...] = total.astype(jnp.bfloat16)


def middle_kernel(near, far, own_out, far_out, mine, theirs, grads_out):
    half = lax.axis_index("h")
    preact = near[...] + far[...].astype(jnp.float32)
    value, slope = gelu_parts(preact)
    value = value.astype(jnp.bfloat16)
    kept = jnp.where(half == 0, value[:16], value[16:])
    mine[...] = kept[:, :768]
    theirs[...] = kept[:, 768:]
    own, other = own_out[...].astype(jnp.float32), far_out[...].astype(jnp.float32)
    low = (jnp.where(half == 0, own, other) * slope[:16]).astype(jnp.bfloat16)
    high = (jnp.where(half == 0, other, own) * slope[16:]).astype(jnp.bfloat16)
    for k in range(8):
        grads_out[k, :16] = low
        grads_out[k, 16:] = high


def pack_kernel(grads, theirs, packed):
    packed[:256] = grads[:, 768:]
    packed[256:] = theirs[...]


def back_kernel(grads, own, *refs):
    *pieces, out = refs
    dims = (((1,), (1,)), ((), ()))
    row = 0
    for piece in pieces:
        rows = piece.shape[0] - 16
        out[:, row : row + rows] = (
            lax.dot_general(
                grads[:, :768], own[row : row + rows], dims, preferred_element_type=jnp.float32
            )
            + lax.dot_general(grads[:, 768:], piece[:rows], dims, preferred_element_type=jnp.float32)
        ).astype(jnp.bfloat16)
        row += rows


def outer_kernel(tokens, grads, mine, other_tokens, other, weight_grad, activated):
    dims = (((0,), (0,)), ((), ()))
    weight_grad[...] = (
        lax.dot_general(tokens[...], grads[:, :768], dims, preferred_element_type=jnp.float32)
        + lax.dot_general(other_tokens[...], other[:256], dims, preferred_element_type=jnp.float32)
    ).astype(jnp.bfloat16)
    core = lax.axis_index("c")
    activated[pl.ds(pl.multiple_of(core * 16, 16), 16), :] = mine[...]
    activated[pl.ds(pl.multiple_of(16 - core * 16, 16), 16), :] = other[256:]


def sum_kernel(parts, out):
    total = parts[0].astype(jnp.float32)
    for k in range(1, 16):
        total += parts[k].astype(jnp.float32)
    out[...] = total.astype(jnp.bfloat16)


def call(kernel, shapes, *operands, flops=0):
    shapes = [jax.ShapeDtypeStruct(s, jnp.bfloat16) if isinstance(s, tuple) else s for s in shapes]
    moved = sum(a.size * a.dtype.itemsize for a in (*operands, *shapes))
    outs = pl.pallas_call(
        kernel,
        out_shape=shapes,
        in_specs=[VMEM] * len(operands),
        out_specs=[VMEM] * len(shapes),
        compiler_params=pltpu.CompilerParams(vmem_limit_bytes=12 * 2**20),
    )(*operands)
    return outs if len(outs) > 1 else outs[0]


def exchange(blocks, axes):
    return lax.all_to_all(blocks, axes, 0, 0, tiled=True)


def swap(block, axis="c"):
    return lax.ppermute(block, axis, SWAP)


def after(value, *others):
    return lax.optimization_barrier((value, *others))[0]


def local(inputs, weight, grad_out):
    copies = jnp.tile(inputs[None], (16, 1, 1))
    tokens = exchange(copies, CHIPS).reshape(256, 768)
    given, sent_weight = after(grad_out, copies), after(weight, copies)
    pieces = [
        swap(jnp.concatenate([sent_weight[384 * k : 384 * k + 384], given[16 * k : 16 * k + 16]]))
        for k in (0, 1)
    ]

    def project(kernel, out, *operands):
        return pl.pallas_call(
            kernel,
            out_shape=out,
            in_specs=[VMEM] * len(operands),
            out_specs=VMEM,
            scratch_shapes=[pltpu.VMEM((128, 768), jnp.bfloat16)],
            compiler_params=pltpu.CompilerParams(vmem_limit_bytes=12 * 2**20),
        )(*operands)

    by_peer = tokens.reshape(8, 32, 768)
    half = jax.ShapeDtypeStruct((128, 768), jnp.bfloat16)
    sent_low = project(low_away_kernel, half, by_peer, weight)
    sent_high = project(high_away_kernel, half, after(by_peer, sent_low), *pieces)
    low = lax.ppermute(sent_low, Y, [(k, k ^ 1) for k in range(8)])
    high = lax.ppermute(sent_high, Y, [(k, (k + (1 if k % 2 else -1)) % 8) for k in range(8)])
    kept = project(
        kept_kernel,
        jax.ShapeDtypeStruct((128, 1536), jnp.float32),
        after(by_peer, sent_high),
        weight,
        *pieces,
    )
    pair_sum = call(pair_kernel, [(128, 1536)], kept, low, high)
    own_out = call(rows_kernel, [(16, 1536)], grad_out, *pieces)
    far_out = swap(after(own_out, pair_sum), "h")
    parts = after(exchange(pair_sum.reshape(4, 32, 1536), ("a",)), far_out)
    near, sent = call(
        add_kernel,
        [jax.ShapeDtypeStruct((32, 1536), jnp.float32), (32, 1536)],
        parts,
    )
    mine, theirs, grad_copies = call(
        middle_kernel,
        [(16, 768), (16, 768), (8, 32, 1536)],
        near, swap(sent, "h"), own_out, far_out,
    )
    grads = exchange(grad_copies, Y).reshape(256, 1536)

    back = call(
        back_kernel, [(256, 768)], grads, weight, *pieces, flops=2 * 256 * 768 * 1536
    )
    input_grad = call(sum_kernel, [(16, 768)], exchange(back.reshape(16, 16, 768), CHIPS))

    packed = call(pack_kernel, [(272, 768)], after(grads, back), theirs)
    weight_grad, activated = call(
        outer_kernel,
        [(768, 768), (32, 768)],
        tokens, grads, mine, swap(after(tokens, back)), swap(packed),
        flops=4 * 256 * 768 * 768,
    )
    return (activated, input_grad, weight_grad)


def solution(mesh):
    fine = Mesh(mesh.devices.reshape(4, 2, 2, 4, 4, 2), ("a", "b", "h", "l", "x", "c"))
    return jax.shard_map(
        local,
        mesh=fine,
        in_specs=(P(COL, ROW), P(ROW, COL), P(ROW, COL)),
        out_specs=(P(ROW, COL), P(COL, ROW), P(ROW, COL)),
        check_vma=False,
    )
```

```python
import jax
import jax.numpy as jnp
from jax import lax
from jax.experimental import pallas as pl
from jax.experimental.pallas import tpu as pltpu
from jax.sharding import Mesh, PartitionSpec as P

coeff = 0.7978845608028654
Y = ("a", "b")
ROW = ("a", "b", "h")
COL = ("l", "x", "c")
CHIPS = ("l", "x")
SWAP = ((0, 1), (1, 0))
VMEM = pl.BlockSpec(memory_space=pltpu.VMEM)


def gelu_parts(preact):
    inner = coeff * (preact + 0.044715 * preact * preact * preact)
    tangent = jnp.tanh(inner)
    value = 0.5 * preact * (1.0 + tangent)
    slope = 0.5 * (1.0 + tangent) + 0.5 * preact * (1.0 - tangent * tangent) * coeff * (
        1.0 + 3.0 * 0.044715 * preact * preact
    )
    return value, slope


def gather_rows(tokens, rows, parity):
    for k in range(4):
        rows[32 * k : 32 * k + 32] = tokens[2 * k + parity]


def high_product(rows, first, second):
    return jnp.dot(rows[:, :384], first[:384], preferred_element_type=jnp.float32) + jnp.dot(
        rows[:, 384:], second[:384], preferred_element_type=jnp.float32
    )


def low_away_kernel(tokens, own, out, rows):
    gather_rows(tokens, rows, 1 - lax.axis_index("b"))
    out[...] = jnp.dot(rows[...], own[...], preferred_element_type=jnp.float32).astype(jnp.bfloat16)


def high_away_kernel(tokens, first, second, out, rows):
    gather_rows(tokens, rows, 1 - lax.axis_index("b"))
    out[...] = high_product(rows, first, second).astype(jnp.bfloat16)


def kept_kernel(tokens, own, first, second, kept, rows):
    gather_rows(tokens, rows, lax.axis_index("b"))
    kept[:, :768] = jnp.dot(rows[...], own[...], preferred_element_type=jnp.float32)
    kept[:, 768:] = high_product(rows, first, second)


def pair_kernel(kept, low, high, out):
    out[:, :768] = (kept[:, :768] + low[...].astype(jnp.float32)).astype(jnp.bfloat16)
    out[:, 768:] = (kept[:, 768:] + high[...].astype(jnp.float32)).astype(jnp.bfloat16)


def rows_kernel(grad_out, first, second, out):
    core = lax.axis_index("c")
    out[:, :768] = jnp.where(core == 0, grad_out[:16], grad_out[16:])
    out[:, 768:] = jnp.where(core == 0, first[-16:], second[-16:])


def add_kernel(parts, wide, narrow):
    total = parts[0].astype(jnp.float32)
    for k in range(1, 4):
        total += parts[k].astype(jnp.float32)
    wide[...] = total
    narrow[...] = total.astype(jnp.bfloat16)


def middle_kernel(near, far, own_out, far_out, mine, theirs, grads_out):
    half = lax.axis_index("h")
    preact = near[...] + far[...].astype(jnp.float32)
    value, slope = gelu_parts(preact)
    value = value.astype(jnp.bfloat16)
    kept = jnp.where(half == 0, value[:16], value[16:])
    mine[...] = kept[:, :768]
    theirs[...] = kept[:, 768:]
    own, other = own_out[...].astype(jnp.float32), far_out[...].astype(jnp.float32)
    low = (jnp.where(half == 0, own, other) * slope[:16]).astype(jnp.bfloat16)
    high = (jnp.where(half == 0, other, own) * slope[16:]).astype(jnp.bfloat16)
    for k in range(8):
        grads_out[k, :16] = low
        grads_out[k, 16:] = high


def pack_kernel(grads, theirs, packed):
    packed[:256] = grads[:, 768:]
    packed[256:] = theirs[...]


def back_kernel(grads, own, *refs):
    *pieces, out = refs
    dims = (((1,), (1,)), ((), ()))
    row = 0
    for piece in pieces:
        rows = piece.shape[0] - 16
        out[:, row : row + rows] = (
            lax.dot_general(
                grads[:, :768], own[row : row + rows], dims, preferred_element_type=jnp.float32
            )
            + lax.dot_general(grads[:, 768:], piece[:rows], dims, preferred_element_type=jnp.float32)
        ).astype(jnp.bfloat16)
        row += rows


def outer_kernel(tokens, grads, mine, other_tokens, other, weight_grad, activated):
    dims = (((0,), (0,)), ((), ()))
    weight_grad[...] = (
        lax.dot_general(tokens[...], grads[:, :768], dims, preferred_element_type=jnp.float32)
        + lax.dot_general(other_tokens[...], other[:256], dims, preferred_element_type=jnp.float32)
    ).astype(jnp.bfloat16)
    core = lax.axis_index("c")
    activated[pl.ds(pl.multiple_of(core * 16, 16), 16), :] = mine[...]
    activated[pl.ds(pl.multiple_of(16 - core * 16, 16), 16), :] = other[256:]


def sum_kernel(parts, out):
    total = parts[0].astype(jnp.float32)
    for k in range(1, 16):
        total += parts[k].astype(jnp.float32)
    out[...] = total.astype(jnp.bfloat16)


def call(kernel, shapes, *operands, flops=0):
    shapes = [jax.ShapeDtypeStruct(s, jnp.bfloat16) if isinstance(s, tuple) else s for s in shapes]
    moved = sum(a.size * a.dtype.itemsize for a in (*operands, *shapes))
    outs = pl.pallas_call(
        kernel,
        out_shape=shapes,
        in_specs=[VMEM] * len(operands),
        out_specs=[VMEM] * len(shapes),
        compiler_params=pltpu.CompilerParams(vmem_limit_bytes=12 * 2**20),
    )(*operands)
    return outs if len(outs) > 1 else outs[0]


def exchange(blocks, axes):
    return lax.all_to_all(blocks, axes, 0, 0, tiled=True)


def swap(block, axis="c"):
    return lax.ppermute(block, axis, SWAP)


def after(value, *others):
    return lax.optimization_barrier((value, *others))[0]


def local(inputs, weight, grad_out):
    copies = jnp.tile(inputs[None], (16, 1, 1))
    tokens = exchange(copies, CHIPS).reshape(256, 768)
    given, sent_weight = after(grad_out, copies), after(weight, copies)
    pieces = [
        swap(jnp.concatenate([sent_weight[384 * k : 384 * k + 384], given[16 * k : 16 * k + 16]]))
        for k in (0, 1)
    ]

    def project(kernel, out, *operands):
        return pl.pallas_call(
            kernel,
            out_shape=out,
            in_specs=[VMEM] * len(operands),
            out_specs=VMEM,
            scratch_shapes=[pltpu.VMEM((128, 768), jnp.bfloat16)],
            compiler_params=pltpu.CompilerParams(vmem_limit_bytes=12 * 2**20),
        )(*operands)

    by_peer = tokens.reshape(8, 32, 768)
    half = jax.ShapeDtypeStruct((128, 768), jnp.bfloat16)
    sent_low = project(low_away_kernel, half, by_peer, weight)
    sent_high = project(high_away_kernel, half, after(by_peer, sent_low), *pieces)
    low = lax.ppermute(sent_low, Y, [(k, k ^ 1) for k in range(8)])
    high = lax.ppermute(sent_high, Y, [(k, (k + (1 if k % 2 else -1)) % 8) for k in range(8)])
    kept = project(
        kept_kernel,
        jax.ShapeDtypeStruct((128, 1536), jnp.float32),
        after(by_peer, sent_high),
        weight,
        *pieces,
    )
    pair_sum = call(pair_kernel, [(128, 1536)], kept, low, high)
    own_out = call(rows_kernel, [(16, 1536)], grad_out, *pieces)
    far_out = swap(after(own_out, pair_sum), "h")
    other_tokens = swap(after(tokens, pair_sum))
    parts = after(exchange(pair_sum.reshape(4, 32, 1536), ("a",)), far_out, other_tokens)
    near, sent = call(
        add_kernel,
        [jax.ShapeDtypeStruct((32, 1536), jnp.float32), (32, 1536)],
        parts,
    )
    mine, theirs, grad_copies = call(
        middle_kernel,
        [(16, 768), (16, 768), (8, 32, 1536)],
        near, swap(sent, "h"), own_out, far_out,
    )
    grads = exchange(grad_copies, Y).reshape(256, 1536)

    back = call(
        back_kernel, [(256, 768)], grads, weight, *pieces, flops=2 * 256 * 768 * 1536
    )
    input_grad = call(sum_kernel, [(16, 768)], exchange(back.reshape(16, 16, 768), CHIPS))

    packed = call(pack_kernel, [(272, 768)], after(grads, back), theirs)
    weight_grad, activated = call(
        outer_kernel,
        [(768, 768), (32, 768)],
        tokens, grads, mine, other_tokens, swap(packed),
        flops=4 * 256 * 768 * 768,
    )
    return (activated, input_grad, weight_grad)


def solution(mesh):
    fine = Mesh(mesh.devices.reshape(4, 2, 2, 4, 4, 2), ("a", "b", "h", "l", "x", "c"))
    return jax.shard_map(
        local,
        mesh=fine,
        in_specs=(P(COL, ROW), P(ROW, COL), P(ROW, COL)),
        out_specs=(P(ROW, COL), P(COL, ROW), P(ROW, COL)),
        check_vma=False,
    )
```
